512 devices in a mesh: dp: 32 (over z, x_hi), row: 8 (over y, core), col: 2 (over x_lo).
Axes of the slice: x: 4 (x_hi: 2, x_lo: 2; x = x_hi * 2 + x_lo), y: 4, z: 16, core: 2. Of those that a mesh axis runs over, the one named last changes fastest.
Arguments:
- counts: int32 [24576, 16384], P('dp', ('row', 'col')), may hold values from 0 to 32, as said below
- coef: float32 [16384, 512], P(('row', 'col'), 'dp'), may hold values from -0.3 to 1.5, as said below
Outputs:
- new_coef: float32 [16384, 512], P(('row', 'col'), 'dp')
- objective: float32 [], replicated
The draws below stay inside these ranges and needn't reach their ends.
Inputs may be any that keep to these rules, and one draw needn't show every extreme that they name: Whole counts. `coef`: diagonal positions hold 0.5 to 1.5.
All inputs are finite; a program needn't handle non-finite values.
Results may differ from the reference program's by a relative error of at most 0.006.
Values may be sent and summed in bfloat16 or wider, within the bound.
No kernel may reach another device: no remote copies, remote signals or barrier semaphores. Data moves between devices by JAX's collectives and lax.ppermute only.
A program may use at most 64 MiB of HBM per device.

```python
import jax
import jax.numpy as jnp
from jax import lax

P_SIZE = 16384
C = 512
CELLS_DEV = 768
N_DP = 32


def draw_counts(key, part):
    key = jax.random.fold_in(key, 11)
    cell_key, gene_key, value_key, keep_key = jax.random.split(key, 4)
    cells_all = CELLS_DEV * N_DP
    cell_level = jax.random.randint(cell_key, (cells_all, 1), 1, 9)
    gene_level = jax.random.randint(gene_key, (1, P_SIZE), 1, 5)
    cell_level = cell_level.at[0, 0].set(8)
    gene_level = gene_level.at[0, 0].set(4)
    values = jax.random.randint(value_key, (cells_all, P_SIZE), 0, cell_level * gene_level + 1)
    position = lax.broadcasted_iota(jnp.int32, (cells_all, 1), 0)
    thresh = 100 + 800 * position // max(cells_all - 1, 1)
    ticket = jax.random.randint(keep_key, (cells_all, P_SIZE), 0, 1000)
    values = jnp.where(ticket < thresh, values, 0)
    return values.at[0, 0].set(32).astype(jnp.int32)


def draw_coef(key, part):
    key = jax.random.fold_in(key, 23)
    off_key, diag_key = jax.random.split(key)
    off = jnp.clip(0.06 * jax.random.normal(off_key, (P_SIZE, C), jnp.float32), -0.3, 0.3)
    diag = jax.random.uniform(diag_key, (P_SIZE, C), jnp.float32, 0.5, 1.5)
    rows_id = lax.broadcasted_iota(jnp.int32, (P_SIZE, C), 0)
    cols_id = lax.broadcasted_iota(jnp.int32, (P_SIZE, C), 1)
    return jnp.where(rows_id == cols_id, diag, off).astype(jnp.float32)


def setup_inputs(seed: int = 0) -> dict:
    keys = jax.random.split(jax.random.key(seed), 3)
    return {
        "counts": draw_counts(jax.random.fold_in(keys[2], 71), 0),
        "coef": draw_coef(jax.random.fold_in(keys[2], 71), 0),
    }


STEP = 0.5
PENALTY = 0.05
SCALE = 10000.0


def reference(counts, coef):
    blocks = 16
    width = P_SIZE // blocks
    total = counts.shape[0]
    index = jnp.arange(blocks, dtype=jnp.int32)

    def piece_of(block):
        start = (block * width).astype(jnp.int32)
        return lax.dynamic_slice_in_dim(counts, start, width, 1).astype(jnp.float32)

    def lib_step(acc, block):
        return acc + jnp.sum(piece_of(block), axis=1), None

    library, unused = lax.scan(lib_step, jnp.zeros((total,), jnp.float32), index)

    def centered_of(block):
        expression = jnp.log1p(SCALE * piece_of(block) / (library[:, None] + 1.0))
        means = jnp.sum(expression, axis=0) / total
        return (expression - means).astype(jnp.bfloat16)

    def proj_step(acc, block):
        start = (block * width).astype(jnp.int32)
        rows = lax.dynamic_slice_in_dim(coef, start, width, 0).astype(jnp.bfloat16)
        term = jnp.dot(centered_of(block).astype(jnp.float32), rows.astype(jnp.float32))
        return acc + term, None

    projection, unused = lax.scan(proj_step, jnp.zeros((total, C), jnp.float32), index)
    projection_low = projection.astype(jnp.bfloat16).astype(jnp.float32)

    def covar_block(block):
        return jnp.dot(centered_of(block).astype(jnp.float32).T, projection_low) / total

    covar_coef = lax.map(covar_block, index).reshape(P_SIZE, C)
    rows_id = lax.broadcasted_iota(jnp.int32, (P_SIZE, C), 0)
    cols_id = lax.broadcasted_iota(jnp.int32, (P_SIZE, C), 1)
    on_diag = rows_id == cols_id
    safe = jnp.where(on_diag, coef, 1.0)
    inverse = jnp.where(on_diag, 1.0 / safe, 0.0)
    gradient = covar_coef - inverse
    stepped = coef - STEP * gradient
    limit = STEP * PENALTY
    shrunk = jnp.where(on_diag, stepped, stepped - jnp.clip(stepped, -limit, limit))
    top = shrunk[:C]
    new_coef = jnp.concatenate([0.5 * (top + top.T), shrunk[C:]], axis=0)
    quad = jnp.sum(projection * projection) / (2.0 * total)
    logsum = jnp.sum(jnp.where(on_diag, jnp.log(safe), 0.0))
    absolute = jnp.sum(jnp.where(on_diag, 0.0, jnp.abs(coef)))
    objective = quad - logsum + PENALTY * absolute
    return new_coef, objective
```

```python
import jax
import jax.numpy as jnp
from jax import lax
from jax.sharding import Mesh, PartitionSpec as P

STEP = 0.5
PENALTY = 0.05
SCALE = 10000.0

FAR = "zh"
NEAR = ("zl", "xh")
TILE = ("y", "core", "xl")
AXES = (FAR,) + NEAR + TILE
SIZES = (8, 2, 2, 4, 2, 2)
N_FAR, N_NEAR, N_TILE = 8, 4, 16
EXTRA = 8


def spread(block, axes, n):
    return lax.all_to_all(jnp.broadcast_to(block[None], (n,) + block.shape), axes, 0, 0)


def split3(v):
    hi = lax.reduce_precision(v, 8, 7)
    rest = v - hi
    mid = lax.reduce_precision(rest, 8, 7)
    return [a.astype(jnp.bfloat16) for a in (hi, mid, rest - mid)]


def join3(rows):
    rows = rows.astype(jnp.float32)
    return (rows[:, 2] + rows[:, 1]) + rows[:, 0]


def outer_sum(left, right):
    return sum(left[i][:, None] * right[i][None, :] for i in range(left.shape[0]))


def extras(means, w, scalars):
    vec = jnp.concatenate([means, w])
    sc = jnp.pad(jnp.stack(scalars), (0, vec.shape[0] - len(scalars)))
    rows = split3(vec) + split3(sc)
    rows += [jnp.zeros_like(rows[0])] * (EXTRA - len(rows))
    return jnp.stack(rows)


def read_extras(rows, genes):
    vec = join3(rows[:, 0:3])
    sc = join3(rows[:, 3:6, :128])
    return vec[:, :genes], vec[:, genes:], [sc[:, i] for i in range(3)]


def per_device(counts, coef):
    cells, genes = counts.shape
    cols = coef.shape[1]
    n_dp = N_FAR * N_NEAR
    band = cols * n_dp
    total = float(cells * n_dp)
    tile = lax.axis_index(TILE)
    near = lax.axis_index(NEAR)
    far = lax.axis_index(FAR)
    part = far * N_NEAR + near
    f32, bf16 = jnp.float32, jnp.bfloat16

    coef_t = coef.T
    w_far = spread(coef_t.astype(bf16), FAR, N_FAR).reshape(N_FAR * cols, genes)
    weights = spread(w_far, NEAR, N_NEAR).reshape(band, genes)

    rows_id = lax.broadcasted_iota(jnp.int32, (cols, genes), 1) + tile * genes
    cols_id = lax.broadcasted_iota(jnp.int32, (cols, genes), 0) + part * cols
    on_diag = rows_id == cols_id
    safe = jnp.where(on_diag, coef_t, 1.0)
    logsum = jnp.sum(jnp.where(on_diag, jnp.log(safe), 0.0))
    absolute = jnp.sum(jnp.where(on_diag, 0.0, jnp.abs(coef_t)))

    lib_rows = cells // 128
    lib = jnp.sum(counts, axis=1).astype(f32).reshape(lib_rows, 128)
    sums = jnp.pad(jnp.stack([logsum, absolute])[None], ((0, 7 - lib_rows % 8), (0, 126)))
    head = jnp.sum(spread(jnp.concatenate([lib, sums]), TILE, N_TILE), axis=0)
    library = head[:lib_rows].reshape(cells)
    logsum, absolute = head[lib_rows, 0], head[lib_rows, 1]

    scale = SCALE / (library + 1.0)
    expr = jnp.log(1.0 + counts.astype(f32) * scale[:, None]).astype(bf16)
    expr = lax.optimization_barrier(expr)
    sums_e = jnp.sum(expr.astype(f32), axis=0)

    partial = lax.dot_general(weights, expr, (((1,), (1,)), ((), ())), preferred_element_type=f32)
    got = lax.all_to_all(partial.astype(bf16).reshape(N_TILE, band // N_TILE, cells), TILE, 0, 0)
    mine = jnp.sum(got.astype(f32), axis=0).astype(bf16)
    proj = spread(mine, TILE, N_TILE).reshape(band, cells)

    proj_f = proj.astype(f32)
    w = jnp.sum(proj_f, axis=1) / cells
    quad = jnp.sum(proj_f * proj_f) - cells * jnp.sum(w * w)
    means = sums_e / cells
    covar = lax.dot_general(proj, expr, (((1,), (0,)), ((), ())), preferred_element_type=f32)
    covar = (covar - w[:, None] * sums_e[None, :]).astype(bf16)
    natural = covar[:, :band].reshape(N_NEAR, N_FAR, cols, band).transpose(1, 0, 2, 3)
    mirror = natural.reshape(band, band).T
    mirror = mirror.reshape(N_FAR, N_NEAR, cols, band).transpose(1, 0, 2, 3)
    main = jnp.concatenate(
        [
            covar.reshape(N_NEAR, N_FAR * cols, genes),
            mirror.reshape(N_NEAR, N_FAR * cols, band),
        ],
        axis=2,
    )
    w_nat = w.reshape(N_NEAR, N_FAR, cols).transpose(1, 0, 2).reshape(band)
    more = extras(means, w_nat, [quad, logsum, absolute])
    more = jnp.broadcast_to(more[None], (N_NEAR,) + more.shape)
    got = lax.all_to_all(jnp.concatenate([main, more], axis=1), NEAR, 0, 0)

    def of_near(v):
        v = v.reshape(-1, N_FAR, N_NEAR, cols)
        return lax.dynamic_index_in_dim(v, near, 2, False).reshape(-1, N_FAR * cols)

    def merge(got, weight, pick):
        n, rows = got.shape[0], got.shape[1] - EXTRA
        means, w, (quad, logsum, absolute) = read_extras(got[:, rows:], genes)
        means_all = jnp.sum(means, axis=0) / n
        w_all = jnp.sum(w, axis=0) / n
        dm, dw = means - means_all, w - w_all
        total_a = jnp.sum(got[:, :rows, :genes].astype(f32), axis=0)
        total_b = jnp.sum(got[:, :rows, genes:].astype(f32), axis=0)
        total_a += outer_sum(pick(dw) * weight, dm)
        total_b += outer_sum(pick(dm[:, :band]) * weight, dw)
        quad = jnp.sum(quad) + weight * jnp.sum(dw * dw)
        return total_a, total_b, means_all, w_all, quad, jnp.sum(logsum), jnp.sum(absolute)

    total_a, total_b, means, w, quad, logsum, absolute = merge(got, float(cells), of_near)
    main = jnp.concatenate([total_a, total_b], axis=1).astype(bf16)
    main = main.reshape(N_FAR, cols, genes + band)
    more = extras(means, w, [quad, logsum, absolute])
    more = jnp.broadcast_to(more[None], (N_FAR,) + more.shape)
    got = lax.all_to_all(jnp.concatenate([main, more], axis=1), FAR, 0, 0)

    def of_part(v):
        return lax.dynamic_slice_in_dim(v, part * cols, cols, 1)

    total_a, total_b, _, _, quad, logsum, absolute = merge(got, float(cells * N_NEAR), of_part)
    inverse = jnp.where(on_diag, 1.0 / safe, 0.0)
    stepped = coef_t - STEP * (total_a / total - inverse)
    limit = STEP * PENALTY
    shrunk = jnp.where(on_diag, stepped, stepped - jnp.clip(stepped, -limit, limit))

    coef_m = lax.dynamic_slice_in_dim(weights, part * cols, cols, 1)
    coef_m = coef_m.reshape(N_NEAR, N_FAR, cols, cols).transpose(1, 0, 2, 3).reshape(band, cols)
    stepped_m = coef_m.T.astype(f32) - STEP * (total_b / total)
    shrunk_m = stepped_m - jnp.clip(stepped_m, -limit, limit)
    top = shrunk[:, :band]
    use = jnp.logical_and(tile == 0, jnp.logical_not(on_diag[:, :band]))
    paired = jnp.where(use, 0.5 * (top + shrunk_m), top)
    new_coef = jnp.concatenate([paired, shrunk[:, band:]], axis=1).T
    objective = quad / (2.0 * total) - logsum + PENALTY * absolute
    return (new_coef, objective)


def solution(mesh):
    mesh = Mesh(mesh.devices.reshape(SIZES), AXES)
    return jax.shard_map(
        per_device,
        mesh=mesh,
        in_specs=(P((FAR,) + NEAR, TILE), P(TILE, (FAR,) + NEAR)),
        out_specs=(P(TILE, (FAR,) + NEAR), P()),
        check_vma=False,
    )
```

```python
import jax
import jax.numpy as jnp
from jax import lax
from jax.sharding import Mesh, PartitionSpec as P

STEP = 0.5
PENALTY = 0.05
SCALE = 10000.0

FAR = "zh"
NEAR = ("zl", "xh")
TILE = ("y", "core", "xl")
AXES = (FAR,) + NEAR + TILE
SIZES = (8, 2, 2, 4, 2, 2)
N_FAR, N_NEAR, N_TILE = 8, 4, 16
EXTRA = 8


def spread(block, axes, n):
    return lax.all_to_all(jnp.broadcast_to(block[None], (n,) + block.shape), axes, 0, 0)


def split3(v):
    hi = lax.reduce_precision(v, 8, 7)
    rest = v - hi
    mid = lax.reduce_precision(rest, 8, 7)
    return [a.astype(jnp.bfloat16) for a in (hi, mid, rest - mid)]


def join3(rows):
    rows = rows.astype(jnp.float32)
    return (rows[:, 2] + rows[:, 1]) + rows[:, 0]


def outer_sum(left, right):
    return sum(left[i][:, None] * right[i][None, :] for i in range(left.shape[0]))


def extras(means, w, scalars):
    vec = jnp.concatenate([means, w])
    sc = jnp.pad(jnp.stack(scalars), (0, vec.shape[0] - len(scalars)))
    rows = split3(vec) + split3(sc)
    rows += [jnp.zeros_like(rows[0])] * (EXTRA - len(rows))
    return jnp.stack(rows)


def read_extras(rows, genes):
    vec = join3(rows[:, 0:3])
    sc = join3(rows[:, 3:6, :128])
    return vec[:, :genes], vec[:, genes:], [sc[:, i] for i in range(3)]


def per_device(counts, coef):
    cells, genes = counts.shape
    cols = coef.shape[1]
    n_dp = N_FAR * N_NEAR
    band = cols * n_dp
    total = float(cells * n_dp)
    tile = lax.axis_index(TILE)
    near = lax.axis_index(NEAR)
    far = lax.axis_index(FAR)
    part = far * N_NEAR + near
    f32, bf16 = jnp.float32, jnp.bfloat16

    coef_t = coef.T
    w_far = spread(coef_t.astype(bf16), FAR, N_FAR).reshape(N_FAR * cols, genes)

    rows_id = lax.broadcasted_iota(jnp.int32, (cols, genes), 1) + tile * genes
    cols_id = lax.broadcasted_iota(jnp.int32, (cols, genes), 0) + part * cols
    on_diag = rows_id == cols_id
    safe = jnp.where(on_diag, coef_t, 1.0)
    logsum = jnp.sum(jnp.where(on_diag, jnp.log(safe), 0.0))
    absolute = jnp.sum(jnp.where(on_diag, 0.0, jnp.abs(coef_t)))

    lib_rows = cells // 128
    lib = jnp.sum(counts, axis=1).astype(f32).reshape(lib_rows, 128)
    sums = jnp.pad(jnp.stack([logsum, absolute])[None], ((0, 7 - lib_rows % 8), (0, 126)))
    head = lax.psum(lax.psum(jnp.concatenate([lib, sums]), "core"), "xl")
    w_far, head = lax.optimization_barrier((w_far, head))
    weights = spread(w_far, NEAR, N_NEAR).reshape(band, genes)
    head = lax.psum(head, "y")
    library = head[:lib_rows].reshape(cells)
    logsum, absolute = head[lib_rows, 0], head[lib_rows, 1]

    scale = SCALE / (library + 1.0)
    expr = jnp.log(1.0 + counts.astype(f32) * scale[:, None]).astype(bf16)
    expr = lax.optimization_barrier(expr)
    sums_e = jnp.sum(expr.astype(f32), axis=0)

    partial = lax.dot_general(weights, expr, (((1,), (1,)), ((), ())), preferred_element_type=f32)
    got = lax.all_to_all(partial.astype(bf16).reshape(N_TILE, band // N_TILE, cells), TILE, 0, 0)
    mine = jnp.sum(got.astype(f32), axis=0).astype(bf16)
    proj = spread(mine, TILE, N_TILE).reshape(band, cells)

    proj_f = proj.astype(f32)
    w = jnp.sum(proj_f, axis=1) / cells
    quad = jnp.sum(proj_f * proj_f) - cells * jnp.sum(w * w)
    means = sums_e / cells
    covar = lax.dot_general(proj, expr, (((1,), (0,)), ((), ())), preferred_element_type=f32)
    covar = (covar - w[:, None] * sums_e[None, :]).astype(bf16)
    natural = covar[:, :band].reshape(N_NEAR, N_FAR, cols, band).transpose(1, 0, 2, 3)
    mirror = natural.reshape(band, band).T
    mirror = mirror.reshape(N_FAR, N_NEAR, cols, band).transpose(1, 0, 2, 3)
    main = jnp.concatenate(
        [
            covar.reshape(N_NEAR, N_FAR * cols, genes),
            mirror.reshape(N_NEAR, N_FAR * cols, band),
        ],
        axis=2,
    )
    w_nat = w.reshape(N_NEAR, N_FAR, cols).transpose(1, 0, 2).reshape(band)
    more = extras(means, w_nat, [quad, logsum, absolute])
    more = jnp.broadcast_to(more[None], (N_NEAR,) + more.shape)
    got = lax.all_to_all(jnp.concatenate([main, more], axis=1), NEAR, 0, 0)

    def of_near(v):
        v = v.reshape(-1, N_FAR, N_NEAR, cols)
        return lax.dynamic_index_in_dim(v, near, 2, False).reshape(-1, N_FAR * cols)

    def merge(got, weight, pick):
        n, rows = got.shape[0], got.shape[1] - EXTRA
        means, w, (quad, logsum, absolute) = read_extras(got[:, rows:], genes)
        means_all = jnp.sum(means, axis=0) / n
        w_all = jnp.sum(w, axis=0) / n
        dm, dw = means - means_all, w - w_all
        total_a = jnp.sum(got[:, :rows, :genes].astype(f32), axis=0)
        total_b = jnp.sum(got[:, :rows, genes:].astype(f32), axis=0)
        total_a += outer_sum(pick(dw) * weight, dm)
        total_b += outer_sum(pick(dm[:, :band]) * weight, dw)
        quad = jnp.sum(quad) + weight * jnp.sum(dw * dw)
        return total_a, total_b, means_all, w_all, quad, jnp.sum(logsum), jnp.sum(absolute)

    total_a, total_b, means, w, quad, logsum, absolute = merge(got, float(cells), of_near)
    main = jnp.concatenate([total_a, total_b], axis=1).astype(bf16)
    main = main.reshape(N_FAR, cols, genes + band)
    more = extras(means, w, [quad, logsum, absolute])
    more = jnp.broadcast_to(more[None], (N_FAR,) + more.shape)
    got = lax.all_to_all(jnp.concatenate([main, more], axis=1), FAR, 0, 0)

    def of_part(v):
        return lax.dynamic_slice_in_dim(v, part * cols, cols, 1)

    total_a, total_b, _, _, quad, logsum, absolute = merge(got, float(cells * N_NEAR), of_part)
    inverse = jnp.where(on_diag, 1.0 / safe, 0.0)
    stepped = coef_t - STEP * (total_a / total - inverse)
    limit = STEP * PENALTY
    shrunk = jnp.where(on_diag, stepped, stepped - jnp.clip(stepped, -limit, limit))

    coef_m = lax.dynamic_slice_in_dim(weights, part * cols, cols, 1)
    coef_m = coef_m.reshape(N_NEAR, N_FAR, cols, cols).transpose(1, 0, 2, 3).reshape(band, cols)
    stepped_m = coef_m.T.astype(f32) - STEP * (total_b / total)
    shrunk_m = stepped_m - jnp.clip(stepped_m, -limit, limit)
    top = shrunk[:, :band]
    use = jnp.logical_and(tile == 0, jnp.logical_not(on_diag[:, :band]))
    paired = jnp.where(use, 0.5 * (top + shrunk_m), top)
    new_coef = jnp.concatenate([paired, shrunk[:, band:]], axis=1).T
    objective = quad / (2.0 * total) - logsum + PENALTY * absolute
    return (new_coef, objective)


def solution(mesh):
    mesh = Mesh(mesh.devices.reshape(SIZES), AXES)
    return jax.shard_map(
        per_device,
        mesh=mesh,
        in_specs=(P((FAR,) + NEAR, TILE), P(TILE, (FAR,) + NEAR)),
        out_specs=(P(TILE, (FAR,) + NEAR), P()),
        check_vma=False,
    )
```

```python
import functools

import jax
import jax.numpy as jnp
from jax import lax
from jax.experimental import pallas as pl
from jax.experimental.pallas import tpu as pltpu
from jax.sharding import Mesh, PartitionSpec as P

STEP = 0.5
PENALTY = 0.05
SCALE = 10000.0

FAR = "zh"
NEAR = ("zl", "xh")
TILE = ("y", "core", "xl")
AXES = (FAR,) + NEAR + TILE
SIZES = (8, 2, 2, 4, 2, 2)
N_FAR, N_NEAR, N_TILE = 8, 4, 16
EXTRA = 16


def spread(block, axes, n):
    return lax.all_to_all(jnp.broadcast_to(block[None], (n,) + block.shape), axes, 0, 0)


def dot(a, b, dims, **kw):
    return lax.dot_general(a, b, ((dims[:1], dims[1:]), ((), ())), preferred_element_type=jnp.float32, **kw)


def split3(v):
    hi = v.astype(jnp.bfloat16)
    rest = v - hi.astype(jnp.float32)
    mid = rest.astype(jnp.bfloat16)
    return [hi, mid, (rest - mid.astype(jnp.float32)).astype(jnp.bfloat16)]


def extra_rows(vec, scalars, rows):
    sc = jnp.concatenate([scalars, jnp.zeros((1, vec.shape[1] - scalars.shape[1]), jnp.float32)], axis=1)
    parts = [p.astype(jnp.float32) for p in split3(vec) + split3(sc)]
    parts.append(jnp.zeros((rows - 6, vec.shape[1]), jnp.float32))
    return jnp.concatenate(parts, axis=0).astype(jnp.bfloat16)


def join3(rows, n, at):
    return jnp.concatenate([r[n + 2 : n + 3, at] + r[n + 1 : n + 2, at] + r[n : n + 1, at] for r in rows], axis=0)


def pack_kernel(proj_ref, expr_ref, sums_ref, head_ref, out_ref):
    band, cells = proj_ref.shape
    genes = expr_ref.shape[1]
    cols = band // (N_FAR * N_NEAR)
    rows = N_FAR * cols
    proj = proj_ref[...]
    sums = sums_ref[...]
    proj_f = proj.astype(jnp.float32)
    w_col = jnp.sum(proj_f, axis=1, keepdims=True) / cells
    w_row = dot(jnp.ones((8, cells), jnp.bfloat16), proj, (1, 1))[:1] / cells
    quad = jnp.sum(proj_f * proj_f) - cells * jnp.sum(w_row * w_row)
    covar = dot(proj, expr_ref[...], (1, 0)) - w_col * sums
    mirror = covar[:, :band].T.astype(jnp.bfloat16)
    covar = covar.astype(jnp.bfloat16)
    lane = lax.broadcasted_iota(jnp.int32, head_ref.shape, 1)
    scalars = head_ref[...] + jnp.where(lane == 2, quad, 0.0)
    more = extra_rows(jnp.concatenate([sums / cells, w_row], axis=1), scalars, EXTRA)
    for k in range(N_NEAR):
        out_ref[k, :rows, :genes] = covar[k * rows : (k + 1) * rows]
        for h in range(N_FAR):
            at = (h * N_NEAR + k) * cols
            out_ref[k, h * cols : (h + 1) * cols, genes:] = mirror[at : at + cols]
        out_ref[k, rows:, :] = more


def merge(got, pick_a, pick_b, weight, genes, rows):
    n = got.shape[0]
    band = got.shape[2] - genes
    more = [got[i, rows:].astype(jnp.float32) for i in range(n)]
    vec = join3(more, 0, slice(None))
    mean = jnp.sum(vec, axis=0, keepdims=True) / n
    diff = vec - mean
    dm, dw = diff[:, :genes], diff[:, genes:]
    terms_w, terms_m = split3(dw), split3(dm[:, :band])
    left_a = sum(dot(t, pick_a, (1, 0)) for t in terms_w)
    left_b = sum(dot(t, pick_b, (1, 0)) for t in terms_m)
    high = lax.Precision.HIGHEST
    total = got[0, :rows].astype(jnp.float32)
    for i in range(1, n):
        total = total + got[i, :rows].astype(jnp.float32)
    total_a = total[:, :genes] + weight * dot(left_a, dm, (0, 0), precision=high)[:rows]
    total_b = total[:, genes:] + weight * dot(left_b, dw, (0, 0), precision=high)[:rows]
    sc = jnp.sum(join3(more, 3, slice(0, 128)), axis=0, keepdims=True)
    lane = lax.broadcasted_iota(jnp.int32, sc.shape, 1)
    sc = sc + jnp.where(lane == 2, weight * jnp.sum(dw * dw), 0.0)
    return total_a, total_b, mean, sc


def near_kernel(weight, genes, got_ref, pick_a_ref, pick_b_ref, out_ref, more_ref):
    rows = got_ref.shape[1] - EXTRA
    a, b, mean, sc = merge(got_ref[...], pick_a_ref[...], pick_b_ref[...], weight, genes, rows)
    a, b = a.astype(jnp.bfloat16), b.astype(jnp.bfloat16)
    cols = rows // N_FAR
    for h in range(N_FAR):
        out_ref[h, :, :genes] = a[h * cols : (h + 1) * cols]
        out_ref[h, :, genes:] = b[h * cols : (h + 1) * cols]
    more_ref[...] = extra_rows(mean, sc, EXTRA)


def far_kernel(weight, total, genes, place_ref, got_ref, pick_a_ref, pick_b_ref, order_ref, coef_ref, mirror_ref, out_ref, obj_ref):
    cols = coef_ref.shape[0]
    band = order_ref.shape[0]
    got = got_ref[...]
    a, b, _, sc = merge(got, pick_a_ref[...], pick_b_ref[...], weight, genes, cols)
    tile, part = place_ref[0], place_ref[1]
    coef = coef_ref[...]
    rows_id = lax.broadcasted_iota(jnp.int32, coef.shape, 1) + tile * genes
    cols_id = lax.broadcasted_iota(jnp.int32, coef.shape, 0) + part * cols
    on_diag = rows_id == cols_id
    inverse = jnp.where(on_diag, 1.0 / jnp.where(on_diag, coef, 1.0), 0.0)
    stepped = coef - STEP * (a / total - inverse)
    limit = STEP * PENALTY
    shrunk = jnp.where(on_diag, stepped, stepped - jnp.clip(stepped, -limit, limit))
    stepped_m = mirror_ref[...] - STEP * (b / total)
    shrunk_m = stepped_m - jnp.clip(stepped_m, -limit, limit)
    shrunk_m = sum(dot(t, order_ref[...], (1, 0)) for t in split3(shrunk_m)[:2])
    top = shrunk[:, :band]
    use = jnp.logical_and(tile == 0, jnp.logical_not(on_diag[:, :band]))
    out_ref[:, :band] = jnp.where(use, 0.5 * (top + shrunk_m), top)
    out_ref[:, band:] = shrunk[:, band:]
    lane = lax.broadcasted_iota(jnp.int32, sc.shape, 1)
    factor = jnp.where(lane == 0, -1.0, jnp.where(lane == 1, PENALTY, jnp.where(lane == 2, 1.0 / (2.0 * total), 0.0)))
    obj_ref[...] = jnp.sum(sc * factor, axis=1, keepdims=True)


def kernel(fn, outs, in_specs=None):
    specs = {} if in_specs is None else {"in_specs": in_specs}
    return pl.pallas_call(
        fn, out_shape=outs, compiler_params=pltpu.CompilerParams(vmem_limit_bytes=48 * 2**20), **specs
    )


def per_device(counts, coef):
    cells, genes = counts.shape
    cols = coef.shape[1]
    n_dp = N_FAR * N_NEAR
    band = cols * n_dp
    total = float(cells * n_dp)
    tile = lax.axis_index(TILE)
    near = lax.axis_index(NEAR)
    far = lax.axis_index(FAR)
    part = far * N_NEAR + near
    f32, bf16 = jnp.float32, jnp.bfloat16

    coef_t = coef.T
    w_far = spread(coef_t.astype(bf16), FAR, N_FAR).reshape(N_FAR * cols, genes)

    rows_id = lax.broadcasted_iota(jnp.int32, (cols, genes), 1) + tile * genes
    cols_id = lax.broadcasted_iota(jnp.int32, (cols, genes), 0) + part * cols
    on_diag = rows_id == cols_id
    safe = jnp.where(on_diag, coef_t, 1.0)
    logsum = jnp.sum(jnp.where(on_diag, jnp.log(safe), 0.0))
    absolute = jnp.sum(jnp.where(on_diag, 0.0, jnp.abs(coef_t)))

    lib_rows = cells // 128
    lib = jnp.sum(counts, axis=1).astype(f32).reshape(lib_rows, 128)
    sums = jnp.pad(jnp.stack([logsum, absolute])[None], ((0, 7 - lib_rows % 8), (0, 126)))
    head = lax.psum(lax.psum(jnp.concatenate([lib, sums]), "core"), "xl")
    w_far, head = lax.optimization_barrier((w_far, head))
    weights = spread(w_far, NEAR, N_NEAR).reshape(band, genes)
    head = lax.psum(head, "y")
    library = head[:lib_rows].reshape(cells)

    scale = SCALE / (library + 1.0)
    expr = jnp.log(1.0 + counts.astype(f32) * scale[:, None]).astype(bf16)
    expr = lax.optimization_barrier(expr)
    sums_e = jnp.sum(expr.astype(f32), axis=0, keepdims=True)

    partial = dot(weights, expr, (1, 1))
    got = lax.all_to_all(partial.astype(bf16).reshape(N_TILE, band // N_TILE, cells), TILE, 0, 0)
    mine = jnp.sum(got.astype(f32), axis=0).astype(bf16)
    proj = spread(mine, TILE, N_TILE).reshape(band, cells)

    rows = N_FAR * cols
    shape = jax.ShapeDtypeStruct((N_NEAR, rows + EXTRA, genes + band), bf16)
    got = kernel(pack_kernel, shape)(proj, expr, sums_e, head[lib_rows : lib_rows + 1])
    got = lax.all_to_all(got, NEAR, 0, 0)

    def onehot(at, n):
        return (lax.broadcasted_iota(jnp.int32, (n, at.shape[0]), 0) == at[None, :]).astype(bf16)

    slot = jnp.arange(rows, dtype=jnp.int32)
    pick_a = onehot(near * rows + slot, band)
    pick_b = onehot((slot // cols * N_NEAR + near) * cols + slot % cols, band)
    shapes = (
        jax.ShapeDtypeStruct((N_FAR, cols, genes + band), bf16),
        jax.ShapeDtypeStruct((EXTRA, genes + band), bf16),
    )
    main, more = kernel(functools.partial(near_kernel, float(cells), genes), shapes)(got, pick_a, pick_b)
    more = jnp.broadcast_to(more[None, :8], (N_FAR, 8, genes + band))
    got = lax.all_to_all(jnp.concatenate([main, more], axis=1), FAR, 0, 0)

    slot = jnp.arange(128, dtype=jnp.int32)
    slot_ok = slot < cols
    pick_a = onehot(jnp.where(slot_ok, near * rows + far * cols + slot, band), band)
    pick_b = onehot(jnp.where(slot_ok, part * cols + slot, band), band)
    nat = jnp.arange(band, dtype=jnp.int32)
    group = nat // cols
    order = onehot((group % N_NEAR * N_FAR + group // N_NEAR) * cols + nat % cols, band)
    here = onehot(part * cols + jnp.arange(cols, dtype=jnp.int32), genes)
    coef_m = dot(here, weights, (0, 1))
    place = jnp.stack([tile, part]).astype(jnp.int32)
    shapes = (jax.ShapeDtypeStruct((cols, genes), f32), jax.ShapeDtypeStruct((1, 1), f32))
    specs = [pl.BlockSpec(memory_space=pltpu.SMEM)] + [pl.BlockSpec(memory_space=pltpu.VMEM)] * 6
    new_t, objective = kernel(
        functools.partial(far_kernel, float(cells * N_NEAR), total, genes), shapes, specs
    )(place, got, pick_a, pick_b, order, coef_t, coef_m)
    return (new_t.T, objective[0, 0])


def solution(mesh):
    mesh = Mesh(mesh.devices.reshape(SIZES), AXES)
    return jax.shard_map(
        per_device,
        mesh=mesh,
        in_specs=(P((FAR,) + NEAR, TILE), P(TILE, (FAR,) + NEAR)),
        out_specs=(P(TILE, (FAR,) + NEAR), P()),
        check_vma=False,
    )
```

```python
import functools

import jax
import jax.numpy as jnp
from jax import lax
from jax.experimental import pallas as pl
from jax.experimental.pallas import tpu as pltpu
from jax.sharding import Mesh, PartitionSpec as P

STEP = 0.5
PENALTY = 0.05
SCALE = 10000.0

FAR = "zh"
NEAR = ("zl", "xh")
TILE = ("y", "core", "xl")
AXES = (FAR,) + NEAR + TILE
SIZES = (8, 2, 2, 4, 2, 2)
N_FAR, N_NEAR, N_TILE = 8, 4, 16
LANES = 128


def spread(block, axes, n):
    return lax.all_to_all(jnp.broadcast_to(block[None], (n,) + block.shape), axes, 0, 0)


def dot(a, b, dims, **kw):
    return lax.dot_general(a, b, ((dims[:1], dims[1:]), ((), ())), preferred_element_type=jnp.float32, **kw)


def split3(v):
    hi = v.astype(jnp.bfloat16)
    rest = v - hi.astype(jnp.float32)
    mid = rest.astype(jnp.bfloat16)
    return [hi, mid, (rest - mid.astype(jnp.float32)).astype(jnp.bfloat16)]


def extra_rows(vec, scalars):
    terms = [t.astype(jnp.float32) for t in split3(vec)[:2]]
    rows = [t[:, i : i + LANES] for t in terms for i in range(0, vec.shape[1], LANES)]
    return rows + [t.astype(jnp.float32) for t in split3(scalars)]


def join_rows(row, n):
    vec = jnp.concatenate([row(n + i) + row(i) for i in range(n)], axis=1)
    return vec, row(2 * n + 2) + row(2 * n + 1) + row(2 * n)


def spread_kernel(block_ref, out_ref):
    block = block_ref[...].astype(jnp.bfloat16)
    for i in range(out_ref.shape[0]):
        out_ref[i] = block


def pack_kernel(proj_ref, expr_ref, sums_ref, head_ref, out_ref):
    band, cells = proj_ref.shape
    genes = expr_ref.shape[1]
    cols = band // (N_FAR * N_NEAR)
    rows = N_FAR * cols
    proj = proj_ref[...]
    sums = sums_ref[...]
    proj_f = proj.astype(jnp.float32)
    w_col = jnp.sum(proj_f, axis=1, keepdims=True) / cells
    w_row = dot(jnp.ones((8, cells), jnp.bfloat16), proj, (1, 1))[:1] / cells
    quad = jnp.sum(proj_f * proj_f) - cells * jnp.sum(w_row * w_row)
    covar = dot(proj, expr_ref[...], (1, 0)) - w_col * sums
    mirror = covar[:, :band].T.astype(jnp.bfloat16)
    covar = covar.astype(jnp.bfloat16)
    lane = lax.broadcasted_iota(jnp.int32, head_ref.shape, 1)
    scalars = head_ref[...] + jnp.where(lane == 2, quad, 0.0)
    more = extra_rows(jnp.concatenate([sums / cells, w_row], axis=1), scalars)
    more.append(jnp.zeros((rows - len(more), LANES), jnp.float32))
    more = jnp.concatenate(more, axis=0).astype(jnp.bfloat16)
    for k in range(N_NEAR):
        out_ref[k, :, :genes] = covar[k * rows : (k + 1) * rows]
        for h in range(N_FAR):
            at = (h * N_NEAR + k) * cols
            out_ref[k, h * cols : (h + 1) * cols, genes : genes + band] = mirror[at : at + cols]
        out_ref[k, :, genes + band :] = more


def merge(got, vec, sc, pick_a, pick_b, weight, genes, band):
    n, rows = got.shape[:2]
    mean = jnp.sum(vec, axis=0, keepdims=True) / n
    diff = vec - mean
    dm, dw = diff[:, :genes], diff[:, genes:]
    terms_w, terms_m = split3(dw), split3(dm[:, :band])
    left_a = sum(dot(t, pick_a, (1, 0)) for t in terms_w)
    left_b = sum(dot(t, pick_b, (1, 0)) for t in terms_m)
    high = lax.Precision.HIGHEST
    total = got[0, :, : genes + band].astype(jnp.float32)
    for i in range(1, n):
        total = total + got[i, :, : genes + band].astype(jnp.float32)
    total_a = total[:, :genes] + weight * dot(left_a, dm, (0, 0), precision=high)[:rows]
    total_b = total[:, genes:] + weight * dot(left_b, dw, (0, 0), precision=high)[:rows]
    sc = jnp.sum(sc, axis=0, keepdims=True)
    lane = lax.broadcasted_iota(jnp.int32, sc.shape, 1)
    sc = sc + jnp.where(lane == 2, weight * jnp.sum(dw * dw), 0.0)
    return total_a, total_b, mean, sc


def near_kernel(weight, genes, got_ref, pick_a_ref, pick_b_ref, out_ref):
    n, rows, wide = got_ref.shape
    both = wide - LANES
    got = got_ref[...]
    more = [got[i, :32, both:].astype(jnp.float32) for i in range(n)]
    vec, sc = join_rows(lambda r: jnp.concatenate([m[r : r + 1] for m in more], axis=0), both // LANES)
    a, b, mean, sc = merge(got, vec, sc, pick_a_ref[...], pick_b_ref[...], weight, genes, both - genes)
    a, b = a.astype(jnp.bfloat16), b.astype(jnp.bfloat16)
    cols = rows // N_FAR
    more = extra_rows(mean, sc)
    more += [jnp.zeros((1, LANES), jnp.float32)] * (2 * cols - len(more))
    more = [jnp.concatenate(more[i : i + cols], axis=0).astype(jnp.bfloat16) for i in (0, cols)]
    for h in range(N_FAR):
        out_ref[h, :, :genes] = a[h * cols : (h + 1) * cols]
        out_ref[h, :, genes:both] = b[h * cols : (h + 1) * cols]
        out_ref[h, :, both : both + LANES] = more[0]
        out_ref[h, :, both + LANES :] = more[1]


def far_kernel(weight, total, genes, place_ref, got_ref, pick_a_ref, pick_b_ref, order_ref, coef_ref, mirror_ref, out_ref, obj_ref):
    cols = coef_ref.shape[0]
    band = order_ref.shape[0]
    got = got_ref[...]
    more = got[:, :, genes + band :].astype(jnp.float32)

    def row(i):
        at = i // cols * LANES
        return more[:, i % cols, at : at + LANES]

    vec, sc = join_rows(row, (genes + band) // LANES)
    a, b, _, sc = merge(got, vec, sc, pick_a_ref[...], pick_b_ref[...], weight, genes, band)
    tile, part = place_ref[0], place_ref[1]
    coef = coef_ref[...]
    rows_id = lax.broadcasted_iota(jnp.int32, coef.shape, 1) + tile * genes
    cols_id = lax.broadcasted_iota(jnp.int32, coef.shape, 0) + part * cols
    on_diag = rows_id == cols_id
    inverse = jnp.where(on_diag, 1.0 / jnp.where(on_diag, coef, 1.0), 0.0)
    stepped = coef - STEP * (a / total - inverse)
    limit = STEP * PENALTY
    shrunk = jnp.where(on_diag, stepped, stepped - jnp.clip(stepped, -limit, limit))
    stepped_m = mirror_ref[...] - STEP * (b / total)
    shrunk_m = stepped_m - jnp.clip(stepped_m, -limit, limit)
    shrunk_m = sum(dot(t, order_ref[...], (1, 0)) for t in split3(shrunk_m)[:2])
    top = shrunk[:, :band]
    use = jnp.logical_and(tile == 0, jnp.logical_not(on_diag[:, :band]))
    out_ref[:, :band] = jnp.where(use, 0.5 * (top + shrunk_m), top)
    out_ref[:, band:] = shrunk[:, band:]
    lane = lax.broadcasted_iota(jnp.int32, sc.shape, 1)
    factor = jnp.where(lane == 0, -1.0, jnp.where(lane == 1, PENALTY, jnp.where(lane == 2, 1.0 / (2.0 * total), 0.0)))
    obj_ref[...] = jnp.sum(sc * factor, axis=1, keepdims=True)


def kernel(fn, outs, in_specs=None):
    specs = {} if in_specs is None else {"in_specs": in_specs}
    return pl.pallas_call(
        fn, out_shape=outs, compiler_params=pltpu.CompilerParams(vmem_limit_bytes=48 * 2**20), **specs
    )


def per_device(counts, coef):
    cells, genes = counts.shape
    cols = coef.shape[1]
    n_dp = N_FAR * N_NEAR
    band = cols * n_dp
    total = float(cells * n_dp)
    tile = lax.axis_index(TILE)
    near = lax.axis_index(NEAR)
    far = lax.axis_index(FAR)
    part = far * N_NEAR + near
    f32, bf16 = jnp.float32, jnp.bfloat16

    coef_t = coef.T
    w_far = kernel(spread_kernel, jax.ShapeDtypeStruct((N_FAR, cols, genes), bf16))(coef_t)
    w_far = lax.all_to_all(w_far, FAR, 0, 0).reshape(N_FAR * cols, genes)

    rows_id = lax.broadcasted_iota(jnp.int32, (cols, genes), 1) + tile * genes
    cols_id = lax.broadcasted_iota(jnp.int32, (cols, genes), 0) + part * cols
    on_diag = rows_id == cols_id
    safe = jnp.where(on_diag, coef_t, 1.0)
    logsum = jnp.sum(jnp.where(on_diag, jnp.log(safe), 0.0))
    absolute = jnp.sum(jnp.where(on_diag, 0.0, jnp.abs(coef_t)))

    lib_rows = cells // 128
    lib = jnp.sum(counts, axis=1).astype(f32).reshape(lib_rows, 128)
    sums = jnp.pad(jnp.stack([logsum, absolute])[None], ((0, 7 - lib_rows % 8), (0, 126)))
    head = lax.psum(lax.psum(jnp.concatenate([lib, sums]), "core"), "xl")
    w_far, head = lax.optimization_barrier((w_far, head))
    weights = spread(w_far, NEAR, N_NEAR).reshape(band, genes)
    head = lax.psum(head, "y")
    library = head[:lib_rows].reshape(cells)

    scale = SCALE / (library + 1.0)
    expr = jnp.log(1.0 + counts.astype(f32) * scale[:, None]).astype(bf16)
    expr = lax.optimization_barrier(expr)
    sums_e = jnp.sum(expr.astype(f32), axis=0, keepdims=True)

    partial = dot(weights, expr, (1, 1))
    got = lax.all_to_all(partial.astype(bf16).reshape(N_TILE, band // N_TILE, cells), TILE, 0, 0)
    mine = jnp.sum(got.astype(f32), axis=0).astype(bf16)
    proj = spread(mine, TILE, N_TILE).reshape(band, cells)

    rows = N_FAR * cols
    shape = jax.ShapeDtypeStruct((N_NEAR, rows, genes + band + LANES), bf16)
    got = kernel(pack_kernel, shape)(proj, expr, sums_e, head[lib_rows : lib_rows + 1])
    got = lax.all_to_all(got, NEAR, 0, 0)

    def onehot(at, n):
        return (lax.broadcasted_iota(jnp.int32, (n, at.shape[0]), 0) == at[None, :]).astype(bf16)

    slot = jnp.arange(rows, dtype=jnp.int32)
    pick_a = onehot(near * rows + slot, band)
    pick_b = onehot((slot // cols * N_NEAR + near) * cols + slot % cols, band)
    shape = jax.ShapeDtypeStruct((N_FAR, cols, genes + band + 2 * LANES), bf16)
    got = kernel(functools.partial(near_kernel, float(cells), genes), shape)(got, pick_a, pick_b)
    got = lax.all_to_all(got, FAR, 0, 0)

    slot = jnp.arange(LANES, dtype=jnp.int32)
    slot_ok = slot < cols
    pick_a = onehot(jnp.where(slot_ok, near * rows + far * cols + slot, band), band)
    pick_b = onehot(jnp.where(slot_ok, part * cols + slot, band), band)
    nat = jnp.arange(band, dtype=jnp.int32)
    group = nat // cols
    order = onehot((group % N_NEAR * N_FAR + group // N_NEAR) * cols + nat % cols, band)
    here = onehot(part * cols + jnp.arange(cols, dtype=jnp.int32), genes)
    coef_m = dot(here, weights, (0, 1))
    place = jnp.stack([tile, part]).astype(jnp.int32)
    shapes = (jax.ShapeDtypeStruct((cols, genes), f32), jax.ShapeDtypeStruct((1, 1), f32))
    specs = [pl.BlockSpec(memory_space=pltpu.SMEM)] + [pl.BlockSpec(memory_space=pltpu.VMEM)] * 6
    new_t, objective = kernel(
        functools.partial(far_kernel, float(cells * N_NEAR), total, genes), shapes, specs
    )(place, got, pick_a, pick_b, order, coef_t, coef_m)
    return (new_t.T, objective[0, 0])


def solution(mesh):
    mesh = Mesh(mesh.devices.reshape(SIZES), AXES)
    return jax.shard_map(
        per_device,
        mesh=mesh,
        in_specs=(P((FAR,) + NEAR, TILE), P(TILE, (FAR,) + NEAR)),
        out_specs=(P(TILE, (FAR,) + NEAR), P()),
        check_vma=False,
    )
```

```python
import functools

import jax
import jax.numpy as jnp
from jax import lax
from jax.experimental import pallas as pl
from jax.experimental.pallas import tpu as pltpu
from jax.sharding import Mesh, PartitionSpec as P

STEP = 0.5
PENALTY = 0.05
SCALE = 10000.0

FAR = "zh"
NEAR = ("zl", "xh")
TILE = ("y", "core", "xl")
AXES = (FAR,) + NEAR + TILE
SIZES = (8, 2, 2, 4, 2, 2)
N_FAR, N_NEAR, N_TILE = 8, 4, 16
LANES = 128


def dot(a, b, dims, **kw):
    return lax.dot_general(a, b, ((dims[:1], dims[1:]), ((), ())), preferred_element_type=jnp.float32, **kw)


def split3(v):
    hi = v.astype(jnp.bfloat16)
    rest = v - hi.astype(jnp.float32)
    mid = rest.astype(jnp.bfloat16)
    return [hi, mid, (rest - mid.astype(jnp.float32)).astype(jnp.bfloat16)]


def extra_rows(vec, scalars):
    terms = [t.astype(jnp.float32) for t in split3(vec)[:2]]
    rows = [t[:, i : i + LANES] for t in terms for i in range(0, vec.shape[1], LANES)]
    return rows + [t.astype(jnp.float32) for t in split3(scalars)]


def join_rows(row, n):
    vec = jnp.concatenate([row(n + i) + row(i) for i in range(n)], axis=1)
    return vec, row(2 * n + 2) + row(2 * n + 1) + row(2 * n)


def spread_kernel(block_ref, out_ref):
    block = block_ref[...]
    if block.ndim == 3:
        block = jnp.sum(block.astype(jnp.float32), axis=0)
    block = block.astype(jnp.bfloat16)
    for i in range(out_ref.shape[0]):
        out_ref[i] = block


def pack_kernel(mirrored, proj_ref, expr_ref, sums_ref, head_ref, out_ref):
    band, cells = proj_ref.shape
    genes = expr_ref.shape[1]
    cols = band // (N_FAR * N_NEAR)
    rows = N_FAR * cols
    proj = proj_ref[...]
    sums = sums_ref[...]
    proj_f = proj.astype(jnp.float32)
    w_col = jnp.sum(proj_f, axis=1, keepdims=True) / cells
    w_row = dot(jnp.ones((8, cells), jnp.bfloat16), proj, (1, 1))[:1] / cells
    quad = jnp.sum(proj_f * proj_f) - cells * jnp.sum(w_row * w_row)
    covar = dot(proj, expr_ref[...], (1, 0)) - w_col * sums
    if mirrored:
        mirror = covar[:, :band].T.astype(jnp.bfloat16)
    covar = covar.astype(jnp.bfloat16)
    lane = lax.broadcasted_iota(jnp.int32, head_ref.shape, 1)
    scalars = head_ref[...] + jnp.where(lane == 2, quad, 0.0)
    more = extra_rows(jnp.concatenate([sums / cells, w_row], axis=1), scalars)
    more.append(jnp.zeros((rows - len(more), LANES), jnp.float32))
    more = jnp.concatenate(more, axis=0).astype(jnp.bfloat16)
    for k in range(N_NEAR):
        out_ref[k, :, :genes] = covar[k * rows : (k + 1) * rows]
        out_ref[k, :, genes : genes + LANES] = more
        if mirrored:
            for h in range(N_FAR):
                at = (h * N_NEAR + k) * cols
                out_ref[k, h * cols : (h + 1) * cols, genes + LANES :] = mirror[at : at + cols]


def merge(got, vec, sc, picks, weight, genes, band):
    n, rows, wide = got.shape
    mean = jnp.sum(vec, axis=0, keepdims=True) / n
    diff = vec - mean
    dm, dw = diff[:, :genes], diff[:, genes:]

    def total(part, left, right, pick):
        left = sum(dot(t, pick, (1, 0)) for t in split3(left))
        out = sum(part[i].astype(jnp.float32) for i in range(n))
        return out + weight * dot(left, right, (0, 0), precision=lax.Precision.HIGHEST)

    totals = [total(got[:, :, :genes], dw, dm, picks[0])]
    if len(picks) == 2:
        totals.append(total(got[:, :, wide - band :], dm[:, :band], dw, picks[1]))
    sc = jnp.sum(sc, axis=0, keepdims=True)
    lane = lax.broadcasted_iota(jnp.int32, sc.shape, 1)
    sc = sc + jnp.where(lane == 2, weight * jnp.sum(dw * dw), 0.0)
    return totals, mean, sc


def near_kernel(weight, genes, got_ref, *refs):
    n, rows, wide = got_ref.shape
    picks, out_ref = [r[...] for r in refs[:-1]], refs[-1]
    band = picks[0].shape[0]
    cols = rows // N_FAR
    got = got_ref[...]
    more = [got[i, :32, genes : genes + LANES].astype(jnp.float32) for i in range(n)]
    vec, sc = join_rows(lambda r: jnp.concatenate([m[r : r + 1] for m in more], axis=0), (genes + band) // LANES)
    totals, mean, sc = merge(got, vec, sc, picks, weight, genes, band)
    more = extra_rows(mean, sc)
    more += [jnp.zeros((1, LANES), jnp.float32)] * (2 * cols - len(more))
    more = [jnp.concatenate(more[i : i + cols], axis=0).astype(jnp.bfloat16) for i in (0, cols)]
    totals = [t.astype(jnp.bfloat16) for t in totals]
    for h in range(N_FAR):
        out_ref[h, :, :genes] = totals[0][h * cols : (h + 1) * cols]
        out_ref[h, :, genes : genes + LANES] = more[0]
        out_ref[h, :, genes + LANES : genes + 2 * LANES] = more[1]
        if len(totals) == 2:
            out_ref[h, :, genes + 2 * LANES :] = totals[1][h * cols : (h + 1) * cols]


def far_kernel(weight, total, place_ref, got_ref, coef_ref, *refs):
    cols, genes = coef_ref.shape
    refs, out_ref, obj_ref = refs[:-2], refs[-2], refs[-1]
    mirrored = len(refs) > 1
    picks = [r[...] for r in (refs[:2] if mirrored else refs)]
    band = picks[0].shape[0]
    got = got_ref[...]
    more = got[:, :, genes : genes + 2 * LANES].astype(jnp.float32)

    def row(i):
        at = i // cols * LANES
        return more[:, i % cols, at : at + LANES]

    vec, sc = join_rows(row, (genes + band) // LANES)
    totals, _, sc = merge(got, vec, sc, picks, weight, genes, band)
    tile, part = place_ref[0], place_ref[1]
    coef = coef_ref[...]
    rows_id = lax.broadcasted_iota(jnp.int32, coef.shape, 1) + tile * genes
    cols_id = lax.broadcasted_iota(jnp.int32, coef.shape, 0) + part * cols
    on_diag = rows_id == cols_id
    inverse = jnp.where(on_diag, 1.0 / jnp.where(on_diag, coef, 1.0), 0.0)
    stepped = coef - STEP * (totals[0] / total - inverse)
    limit = STEP * PENALTY
    shrunk = jnp.where(on_diag, stepped, stepped - jnp.clip(stepped, -limit, limit))
    out_ref[...] = shrunk
    if mirrored:
        order_ref, mirror_ref = refs[2:]
        stepped_m = mirror_ref[...] - STEP * (totals[1] / total)
        shrunk_m = stepped_m - jnp.clip(stepped_m, -limit, limit)
        shrunk_m = sum(dot(t, order_ref[...], (1, 0)) for t in split3(shrunk_m)[:2])
        top = shrunk[:, :band]
        out_ref[:, :band] = jnp.where(on_diag[:, :band], top, 0.5 * (top + shrunk_m))
    lane = lax.broadcasted_iota(jnp.int32, sc.shape, 1)
    factor = jnp.where(lane == 0, -1.0, jnp.where(lane == 1, PENALTY, jnp.where(lane == 2, 1.0 / (2.0 * total), 0.0)))
    obj_ref[...] = jnp.sum(sc * factor, axis=1, keepdims=True)


def kernel(fn, outs, in_specs=None):
    specs = {} if in_specs is None else {"in_specs": in_specs}
    return pl.pallas_call(
        fn, out_shape=outs, compiler_params=pltpu.CompilerParams(vmem_limit_bytes=48 * 2**20), **specs
    )


def spread(block, axes, n):
    shape = jax.ShapeDtypeStruct((n,) + block.shape[-2:], jnp.bfloat16)
    return lax.all_to_all(kernel(spread_kernel, shape)(block), axes, 0, 0)


def per_device(counts, coef):
    cells, genes = counts.shape
    cols = coef.shape[1]
    n_dp = N_FAR * N_NEAR
    band = cols * n_dp
    total = float(cells * n_dp)
    tile = lax.axis_index(TILE)
    near = lax.axis_index(NEAR)
    far = lax.axis_index(FAR)
    part = far * N_NEAR + near
    f32, bf16 = jnp.float32, jnp.bfloat16

    coef_t = coef.T
    w_far = spread(coef_t, FAR, N_FAR).reshape(N_FAR * cols, genes)

    rows_id = lax.broadcasted_iota(jnp.int32, (cols, genes), 1) + tile * genes
    cols_id = lax.broadcasted_iota(jnp.int32, (cols, genes), 0) + part * cols
    on_diag = rows_id == cols_id
    safe = jnp.where(on_diag, coef_t, 1.0)
    logsum = jnp.sum(jnp.where(on_diag, jnp.log(safe), 0.0))
    absolute = jnp.sum(jnp.where(on_diag, 0.0, jnp.abs(coef_t)))

    lib_rows = cells // 128
    lib = jnp.sum(counts, axis=1).astype(f32).reshape(lib_rows, 128)
    sums = jnp.pad(jnp.stack([logsum, absolute])[None], ((0, 7 - lib_rows % 8), (0, 126)))
    head = lax.psum(jnp.concatenate([lib, sums]), "y")
    w_far, head = lax.optimization_barrier((w_far, head))
    weights = spread(w_far, NEAR, N_NEAR).reshape(band, genes)
    head = lax.psum(lax.psum(head, "core"), "xl")
    library = head[:lib_rows].reshape(cells)

    scale = SCALE / (library + 1.0)
    expr = jnp.log(1.0 + counts.astype(f32) * scale[:, None]).astype(bf16)
    expr = lax.optimization_barrier(expr)
    sums_e = jnp.sum(expr.astype(f32), axis=0, keepdims=True)

    partial = dot(weights, expr, (1, 1))
    got = lax.all_to_all(partial.astype(bf16).reshape(N_TILE, band // N_TILE, cells), TILE, 0, 0)
    proj = spread(got, TILE, N_TILE).reshape(band, cells)

    head = head[lib_rows : lib_rows + 1]
    rows = N_FAR * cols

    def onehot(at, n):
        return (lax.broadcasted_iota(jnp.int32, (n, at.shape[0]), 0) == at[None, :]).astype(bf16)

    def tail(mirrored):
        wide = genes + (band if mirrored else 0)
        n_picks = 2 if mirrored else 1
        shape = jax.ShapeDtypeStruct((N_NEAR, rows, wide + LANES), bf16)
        got = kernel(functools.partial(pack_kernel, mirrored), shape)(proj, expr, sums_e, head)
        got = lax.all_to_all(got, NEAR, 0, 0)

        slot = jnp.arange(rows, dtype=jnp.int32)
        picks = [near * rows + slot, (slot // cols * N_NEAR + near) * cols + slot % cols]
        picks = [onehot(p, band) for p in picks[:n_picks]]
        shape = jax.ShapeDtypeStruct((N_FAR, cols, wide + 2 * LANES), bf16)
        got = kernel(functools.partial(near_kernel, float(cells), genes), shape)(got, *picks)
        got = lax.all_to_all(got, FAR, 0, 0)

        slot = jnp.arange(cols, dtype=jnp.int32)
        more = [onehot(p + slot, band) for p in (near * rows + far * cols, part * cols)[:n_picks]]
        if mirrored:
            nat = jnp.arange(band, dtype=jnp.int32)
            group = nat // cols
            more.append(onehot((group % N_NEAR * N_FAR + group // N_NEAR) * cols + nat % cols, band))
            more.append(dot(onehot(part * cols + slot, genes), weights, (0, 1)))
        place = jnp.stack([tile, part]).astype(jnp.int32)
        shapes = (jax.ShapeDtypeStruct((cols, genes), f32), jax.ShapeDtypeStruct((1, 1), f32))
        specs = [pl.BlockSpec(memory_space=pltpu.SMEM)] + [pl.BlockSpec(memory_space=pltpu.VMEM)] * (2 + len(more))
        return kernel(functools.partial(far_kernel, float(cells * N_NEAR), total), shapes, specs)(
            place, got, coef_t, *more
        )

    new_t, objective = lax.cond(tile == 0, lambda: tail(True), lambda: tail(False))
    return (new_t.T, objective[0, 0])


def solution(mesh):
    mesh = Mesh(mesh.devices.reshape(SIZES), AXES)
    return jax.shard_map(
        per_device,
        mesh=mesh,
        in_specs=(P((FAR,) + NEAR, TILE), P(TILE, (FAR,) + NEAR)),
        out_specs=(P(TILE, (FAR,) + NEAR), P()),
        check_vma=False,
    )
```

```python
import functools

import jax
import jax.numpy as jnp
from jax import lax
from jax.experimental import pallas as pl
from jax.experimental.pallas import tpu as pltpu
from jax.sharding import Mesh, PartitionSpec as P

STEP = 0.5
PENALTY = 0.05
SCALE = 10000.0

FAR = "zh"
NEAR = ("zl", "xh")
TILE = ("y", "core", "xl")
AXES = (FAR,) + NEAR + TILE
SIZES = (8, 2, 2, 4, 2, 2)
N_FAR, N_NEAR, N_TILE = 8, 4, 16
LANES = 128


def dot(a, b, dims, **kw):
    return lax.dot_general(a, b, ((dims[:1], dims[1:]), ((), ())), preferred_element_type=jnp.float32, **kw)


def split3(v):
    hi = v.astype(jnp.bfloat16)
    rest = v - hi.astype(jnp.float32)
    mid = rest.astype(jnp.bfloat16)
    return [hi, mid, (rest - mid.astype(jnp.float32)).astype(jnp.bfloat16)]


def extra_rows(vec, scalars):
    terms = [t.astype(jnp.float32) for t in split3(vec)[:2]]
    rows = [t[:, i : i + LANES] for t in terms for i in range(0, vec.shape[1], LANES)]
    return rows + [t.astype(jnp.float32) for t in split3(scalars)]


def join_rows(row, n):
    vec = jnp.concatenate([row(n + i) + row(i) for i in range(n)], axis=1)
    return vec, row(2 * n + 2) + row(2 * n + 1) + row(2 * n)


def spread_kernel(block_ref, out_ref):
    block = block_ref[...]
    if block.ndim == 3:
        block = jnp.sum(block.astype(jnp.float32), axis=0)
    block = block.astype(jnp.bfloat16)
    for i in range(out_ref.shape[0]):
        out_ref[i] = block


def pack_kernel(mirrored, proj_ref, expr_ref, sums_ref, head_ref, out_ref):
    band, cells = proj_ref.shape
    genes = expr_ref.shape[1]
    cols = band // (N_FAR * N_NEAR)
    rows = N_FAR * cols
    proj = proj_ref[...]
    sums = sums_ref[...]
    proj_f = proj.astype(jnp.float32)
    w_col = jnp.sum(proj_f, axis=1, keepdims=True) / cells
    w_row = dot(jnp.ones((8, cells), jnp.bfloat16), proj, (1, 1))[:1] / cells
    quad = jnp.sum(proj_f * proj_f) - cells * jnp.sum(w_row * w_row)
    covar = dot(proj, expr_ref[...], (1, 0)) - w_col * sums
    if mirrored:
        mirror = covar[:, :band].T.astype(jnp.bfloat16)
    covar = covar.astype(jnp.bfloat16)
    lane = lax.broadcasted_iota(jnp.int32, head_ref.shape, 1)
    scalars = head_ref[...] + jnp.where(lane == 2, quad, 0.0)
    more = extra_rows(jnp.concatenate([sums / cells, w_row], axis=1), scalars)
    more.append(jnp.zeros((rows - len(more), LANES), jnp.float32))
    more = jnp.concatenate(more, axis=0).astype(jnp.bfloat16)
    for k in range(N_NEAR):
        out_ref[k, :, :genes] = covar[k * rows : (k + 1) * rows]
        out_ref[k, :, genes : genes + LANES] = more
        if mirrored:
            for h in range(N_FAR):
                at = (h * N_NEAR + k) * cols
                out_ref[k, h * cols : (h + 1) * cols, genes + LANES :] = mirror[at : at + cols]


def merge(got, vec, sc, picks, weight, genes, band):
    n, rows, wide = got.shape
    mean = jnp.sum(vec, axis=0, keepdims=True) / n
    diff = vec - mean
    dm, dw = diff[:, :genes], diff[:, genes:]

    def total(part, left, right, pick):
        left = sum(dot(t, pick, (1, 0)) for t in split3(left))
        out = sum(part[i].astype(jnp.float32) for i in range(n))
        return out + weight * dot(left, right, (0, 0), precision=lax.Precision.HIGHEST)

    totals = [total(got[:, :, :genes], dw, dm, picks[0])]
    if len(picks) == 2:
        totals.append(total(got[:, :, wide - band :], dm[:, :band], dw, picks[1]))
    sc = jnp.sum(sc, axis=0, keepdims=True)
    lane = lax.broadcasted_iota(jnp.int32, sc.shape, 1)
    sc = sc + jnp.where(lane == 2, weight * jnp.sum(dw * dw), 0.0)
    return totals, mean, sc


def near_kernel(weight, genes, got_ref, *refs):
    n, rows, wide = got_ref.shape
    picks, out_ref = [r[...] for r in refs[:-1]], refs[-1]
    band = picks[0].shape[0]
    cols = rows // N_FAR
    got = got_ref[...]
    more = [got[i, :32, genes : genes + LANES].astype(jnp.float32) for i in range(n)]
    vec, sc = join_rows(lambda r: jnp.concatenate([m[r : r + 1] for m in more], axis=0), (genes + band) // LANES)
    totals, mean, sc = merge(got, vec, sc, picks, weight, genes, band)
    more = extra_rows(mean, sc)
    more += [jnp.zeros((1, LANES), jnp.float32)] * (2 * cols - len(more))
    more = [jnp.concatenate(more[i : i + cols], axis=0).astype(jnp.bfloat16) for i in (0, cols)]
    totals = [t.astype(jnp.bfloat16) for t in totals]
    for h in range(N_FAR):
        out_ref[h, :, :genes] = totals[0][h * cols : (h + 1) * cols]
        out_ref[h, :, genes : genes + LANES] = more[0]
        out_ref[h, :, genes + LANES : genes + 2 * LANES] = more[1]
        if len(totals) == 2:
            out_ref[h, :, genes + 2 * LANES :] = totals[1][h * cols : (h + 1) * cols]


def far_kernel(weight, total, place_ref, got_ref, coef_ref, *refs):
    cols, genes = coef_ref.shape
    refs, out_ref, obj_ref = refs[:-2], refs[-2], refs[-1]
    mirrored = len(refs) > 1
    picks = [r[...] for r in (refs[:2] if mirrored else refs)]
    band = picks[0].shape[0]
    got = got_ref[...]
    more = got[:, :, genes : genes + 2 * LANES].astype(jnp.float32)

    def row(i):
        at = i // cols * LANES
        return more[:, i % cols, at : at + LANES]

    vec, sc = join_rows(row, (genes + band) // LANES)
    totals, _, sc = merge(got, vec, sc, picks, weight, genes, band)
    tile, part = place_ref[0], place_ref[1]
    coef = coef_ref[...]
    rows_id = lax.broadcasted_iota(jnp.int32, coef.shape, 1) + tile * genes
    cols_id = lax.broadcasted_iota(jnp.int32, coef.shape, 0) + part * cols
    on_diag = rows_id == cols_id
    inverse = jnp.where(on_diag, 1.0 / jnp.where(on_diag, coef, 1.0), 0.0)
    stepped = coef - STEP * (totals[0] / total - inverse)
    limit = STEP * PENALTY
    shrunk = jnp.where(on_diag, stepped, stepped - jnp.clip(stepped, -limit, limit))
    out_ref[...] = shrunk
    if mirrored:
        order_ref, mirror_ref = refs[2:]
        stepped_m = mirror_ref[...] - STEP * (totals[1] / total)
        shrunk_m = stepped_m - jnp.clip(stepped_m, -limit, limit)
        shrunk_m = sum(dot(t, order_ref[...], (1, 0)) for t in split3(shrunk_m)[:2])
        top = shrunk[:, :band]
        out_ref[:, :band] = jnp.where(on_diag[:, :band], top, 0.5 * (top + shrunk_m))
    lane = lax.broadcasted_iota(jnp.int32, sc.shape, 1)
    factor = jnp.where(lane == 0, -1.0, jnp.where(lane == 1, PENALTY, jnp.where(lane == 2, 1.0 / (2.0 * total), 0.0)))
    obj_ref[...] = jnp.sum(sc * factor, axis=1, keepdims=True)


def kernel(fn, outs, in_specs=None):
    specs = {} if in_specs is None else {"in_specs": in_specs}
    return pl.pallas_call(
        fn, out_shape=outs, compiler_params=pltpu.CompilerParams(vmem_limit_bytes=24 * 2**20), **specs
    )


def spread(block, axes, n):
    shape = jax.ShapeDtypeStruct((n,) + block.shape[-2:], jnp.bfloat16)
    return lax.all_to_all(kernel(spread_kernel, shape)(block), axes, 0, 0)


def per_device(counts, coef):
    cells, genes = counts.shape
    cols = coef.shape[1]
    n_dp = N_FAR * N_NEAR
    band = cols * n_dp
    total = float(cells * n_dp)
    tile = lax.axis_index(TILE)
    near = lax.axis_index(NEAR)
    far = lax.axis_index(FAR)
    part = far * N_NEAR + near
    f32, bf16 = jnp.float32, jnp.bfloat16

    coef_t = coef.T
    w_far = spread(coef_t, FAR, N_FAR).reshape(N_FAR * cols, genes)

    rows_id = lax.broadcasted_iota(jnp.int32, (cols, genes), 1) + tile * genes
    cols_id = lax.broadcasted_iota(jnp.int32, (cols, genes), 0) + part * cols
    on_diag = rows_id == cols_id
    safe = jnp.where(on_diag, coef_t, 1.0)
    logsum = jnp.sum(jnp.where(on_diag, jnp.log(safe), 0.0))
    absolute = jnp.sum(jnp.where(on_diag, 0.0, jnp.abs(coef_t)))

    lib_rows = cells // 128
    lib = jnp.sum(counts, axis=1).astype(f32).reshape(lib_rows, 128)
    sums = jnp.pad(jnp.stack([logsum, absolute])[None], ((0, 7 - lib_rows % 8), (0, 126)))
    head = lax.psum(lax.psum(jnp.concatenate([lib, sums]), "y"), "core")
    low, w_far, head = lax.optimization_barrier((counts.astype(bf16), w_far, head))
    weights = spread(w_far, NEAR, N_NEAR).reshape(band, genes)
    head = lax.psum(head, "xl")
    library = head[:lib_rows].reshape(cells)

    scale = SCALE / (library + 1.0)
    expr = jnp.log(1.0 + low.astype(f32) * scale[:, None]).astype(bf16)
    expr = lax.optimization_barrier(expr)
    sums_e = jnp.sum(expr.astype(f32), axis=0, keepdims=True)

    partial = dot(weights, expr, (1, 1))
    got = lax.all_to_all(partial.astype(bf16).reshape(N_TILE, band // N_TILE, cells), TILE, 0, 0)
    proj = spread(got, TILE, N_TILE).reshape(band, cells)

    head = head[lib_rows : lib_rows + 1]
    rows = N_FAR * cols

    def onehot(at, n):
        return (lax.broadcasted_iota(jnp.int32, (n, at.shape[0]), 0) == at[None, :]).astype(bf16)

    def tail(mirrored):
        wide = genes + (band if mirrored else 0)
        n_picks = 2 if mirrored else 1
        shape = jax.ShapeDtypeStruct((N_NEAR, rows, wide + LANES), bf16)
        got = kernel(functools.partial(pack_kernel, mirrored), shape)(proj, expr, sums_e, head)
        got = lax.all_to_all(got, NEAR, 0, 0)

        slot = jnp.arange(rows, dtype=jnp.int32)
        picks = [near * rows + slot, (slot // cols * N_NEAR + near) * cols + slot % cols]
        picks = [onehot(p, band) for p in picks[:n_picks]]
        shape = jax.ShapeDtypeStruct((N_FAR, cols, wide + 2 * LANES), bf16)
        got = kernel(functools.partial(near_kernel, float(cells), genes), shape)(got, *picks)
        got = lax.all_to_all(got, FAR, 0, 0)

        slot = jnp.arange(cols, dtype=jnp.int32)
        more = [onehot(p + slot, band) for p in (near * rows + far * cols, part * cols)[:n_picks]]
        if mirrored:
            nat = jnp.arange(band, dtype=jnp.int32)
            group = nat // cols
            more.append(onehot((group % N_NEAR * N_FAR + group // N_NEAR) * cols + nat % cols, band))
            more.append(dot(onehot(part * cols + slot, genes), weights, (0, 1)))
        place = jnp.stack([tile, part]).astype(jnp.int32)
        shapes = (jax.ShapeDtypeStruct((cols, genes), f32), jax.ShapeDtypeStruct((1, 1), f32))
        specs = [pl.BlockSpec(memory_space=pltpu.SMEM)] + [pl.BlockSpec(memory_space=pltpu.VMEM)] * (2 + len(more))
        return kernel(functools.partial(far_kernel, float(cells * N_NEAR), total), shapes, specs)(
            place, got, coef_t, *more
        )

    new_t, objective = lax.cond(tile == 0, lambda: tail(True), lambda: tail(False))
    return (new_t.T, objective[0, 0])


def solution(mesh):
    mesh = Mesh(mesh.devices.reshape(SIZES), AXES)
    return jax.shard_map(
        per_device,
        mesh=mesh,
        in_specs=(P((FAR,) + NEAR, TILE), P(TILE, (FAR,) + NEAR)),
        out_specs=(P(TILE, (FAR,) + NEAR), P()),
        check_vma=False,
    )
```

```python
import functools

import jax
import jax.numpy as jnp
from jax import lax
from jax.experimental import pallas as pl
from jax.experimental.pallas import tpu as pltpu
from jax.sharding import Mesh, PartitionSpec as P

STEP = 0.5
PENALTY = 0.05
SCALE = 10000.0

FAR = "zh"
NEAR = ("zl", "xh")
TILE = ("y", "core", "xl")
AXES = (FAR,) + NEAR + TILE
SIZES = (8, 2, 2, 4, 2, 2)
N_FAR, N_NEAR, N_TILE = 8, 4, 16
LANES = 128


def dot(a, b, dims, **kw):
    return lax.dot_general(a, b, ((dims[:1], dims[1:]), ((), ())), preferred_element_type=jnp.float32, **kw)


def split3(v):
    hi = v.astype(jnp.bfloat16)
    rest = v - hi.astype(jnp.float32)
    mid = rest.astype(jnp.bfloat16)
    return [hi, mid, (rest - mid.astype(jnp.float32)).astype(jnp.bfloat16)]


def extra_rows(vec, scalars):
    terms = [t.astype(jnp.float32) for t in split3(vec)[:2]]
    rows = [t[:, i : i + LANES] for t in terms for i in range(0, vec.shape[1], LANES)]
    return rows + [t.astype(jnp.float32) for t in split3(scalars)]


def join_rows(row, n):
    vec = jnp.concatenate([row(n + i) + row(i) for i in range(n)], axis=1)
    return vec, row(2 * n + 2) + row(2 * n + 1) + row(2 * n)


def diagonal(shape, place_ref):
    rows_id = lax.broadcasted_iota(jnp.int32, shape, 1) + place_ref[0] * shape[1]
    cols_id = lax.broadcasted_iota(jnp.int32, shape, 0) + place_ref[1] * shape[0]
    return rows_id == cols_id


def head_kernel(place_ref, counts_ref, coef_ref, head_ref, low_ref):
    step = pl.program_id(0)
    per_step = counts_ref.shape[0] // LANES

    @pl.when(step == 0)
    def _():
        coef = coef_ref[...]
        on_diag = diagonal(coef.shape, place_ref)
        logsum = jnp.sum(jnp.where(on_diag, jnp.log(jnp.where(on_diag, coef, 1.0)), 0.0))
        absolute = jnp.sum(jnp.where(on_diag, 0.0, jnp.abs(coef)))
        at = lax.broadcasted_iota(jnp.int32, head_ref.shape, 0)
        lane = lax.broadcasted_iota(jnp.int32, head_ref.shape, 1)
        row = jnp.where(lane == 0, logsum, jnp.where(lane == 1, absolute, 0.0))
        head_ref[...] = jnp.where(at == pl.num_programs(0) * per_step, row, 0.0)

    for i in range(per_step):
        rows = slice(i * LANES, (i + 1) * LANES)
        low = counts_ref[rows].astype(jnp.float32).astype(jnp.bfloat16)
        low_ref[rows] = low
        sums = dot(jnp.ones((8, low.shape[1]), jnp.bfloat16), low, (1, 1))
        head_ref[pl.ds(step * per_step + i, 1), :] = sums[:1]


def project_kernel(weights_ref, expr_ref, out_ref):
    out_ref[...] = dot(weights_ref[...], expr_ref[...], (1, 1)).astype(jnp.bfloat16)


def spread_kernel(block_ref, out_ref):
    block = block_ref[...]
    if block.ndim == 3:
        block = jnp.sum(block.astype(jnp.float32), axis=0)
    block = block.astype(jnp.bfloat16)
    for i in range(out_ref.shape[0]):
        out_ref[i] = block


def pack_kernel(mirrored, proj_ref, expr_ref, sums_ref, head_ref, out_ref):
    band, cells = proj_ref.shape
    genes = expr_ref.shape[1]
    cols = band // (N_FAR * N_NEAR)
    rows = N_FAR * cols
    proj = proj_ref[...]
    sums = sums_ref[...]
    proj_f = proj.astype(jnp.float32)
    w_col = jnp.sum(proj_f, axis=1, keepdims=True) / cells
    w_row = dot(jnp.ones((8, cells), jnp.bfloat16), proj, (1, 1))[:1] / cells
    quad = jnp.sum(proj_f * proj_f) - cells * jnp.sum(w_row * w_row)
    covar = dot(proj, expr_ref[...], (1, 0)) - w_col * sums
    if mirrored:
        mirror = covar[:, :band].T.astype(jnp.bfloat16)
    covar = covar.astype(jnp.bfloat16)
    lane = lax.broadcasted_iota(jnp.int32, head_ref.shape, 1)
    scalars = head_ref[...] + jnp.where(lane == 2, quad, 0.0)
    more = extra_rows(jnp.concatenate([sums / cells, w_row], axis=1), scalars)
    more.append(jnp.zeros((rows - len(more), LANES), jnp.float32))
    more = jnp.concatenate(more, axis=0).astype(jnp.bfloat16)
    for k in range(N_NEAR):
        out_ref[k, :, :genes] = covar[k * rows : (k + 1) * rows]
        out_ref[k, :, genes : genes + LANES] = more
        if mirrored:
            for h in range(N_FAR):
                at = (h * N_NEAR + k) * cols
                out_ref[k, h * cols : (h + 1) * cols, genes + LANES :] = mirror[at : at + cols]


def merge(got, vec, sc, picks, weight, genes, band):
    n, rows, wide = got.shape
    mean = jnp.sum(vec, axis=0, keepdims=True) / n
    diff = vec - mean
    dm, dw = diff[:, :genes], diff[:, genes:]

    def total(part, left, right, pick):
        left = weight * sum(dot(pick, t, (1, 1)) for t in split3(left))
        out = sum(part[i].astype(jnp.float32) for i in range(n))
        return out + sum(left[:, i : i + 1] * right[i : i + 1] for i in range(n))

    totals = [total(got[:, :, :genes], dw, dm, picks[0])]
    if len(picks) == 2:
        totals.append(total(got[:, :, wide - band :], dm[:, :band], dw, picks[1]))
    sc = jnp.sum(sc, axis=0, keepdims=True)
    lane = lax.broadcasted_iota(jnp.int32, sc.shape, 1)
    sc = sc + jnp.where(lane == 2, weight * jnp.sum(dw * dw), 0.0)
    return totals, mean, sc


def near_kernel(weight, genes, got_ref, *refs):
    n, rows, wide = got_ref.shape
    picks, out_ref = [r[...] for r in refs[:-1]], refs[-1]
    band = picks[0].shape[1]
    cols = rows // N_FAR
    got = got_ref[...]
    more = [got[i, :32, genes : genes + LANES].astype(jnp.float32) for i in range(n)]
    vec, sc = join_rows(lambda r: jnp.concatenate([m[r : r + 1] for m in more], axis=0), (genes + band) // LANES)
    totals, mean, sc = merge(got, vec, sc, picks, weight, genes, band)
    more = extra_rows(mean, sc)
    more += [jnp.zeros((1, LANES), jnp.float32)] * (2 * cols - len(more))
    more = [jnp.concatenate(more[i : i + cols], axis=0).astype(jnp.bfloat16) for i in (0, cols)]
    totals = [t.astype(jnp.bfloat16) for t in totals]
    for h in range(N_FAR):
        out_ref[h, :, :genes] = totals[0][h * cols : (h + 1) * cols]
        out_ref[h, :, genes : genes + LANES] = more[0]
        out_ref[h, :, genes + LANES : genes + 2 * LANES] = more[1]
        if len(totals) == 2:
            out_ref[h, :, genes + 2 * LANES :] = totals[1][h * cols : (h + 1) * cols]


def far_kernel(weight, total, place_ref, got_ref, coef_ref, *refs):
    cols, genes = coef_ref.shape
    refs, out_ref, obj_ref = refs[:-2], refs[-2], refs[-1]
    mirrored = len(refs) > 1
    picks = [r[...] for r in (refs[:2] if mirrored else refs)]
    band = picks[0].shape[1]
    got = got_ref[...]
    more = got[:, :, genes : genes + 2 * LANES].astype(jnp.float32)

    def row(i):
        at = i // cols * LANES
        return more[:, i % cols, at : at + LANES]

    vec, sc = join_rows(row, (genes + band) // LANES)
    totals, _, sc = merge(got, vec, sc, picks, weight, genes, band)
    coef = coef_ref[...]
    on_diag = diagonal(coef.shape, place_ref)
    inverse = jnp.where(on_diag, 1.0 / jnp.where(on_diag, coef, 1.0), 0.0)
    stepped = coef - STEP * (totals[0] / total - inverse)
    limit = STEP * PENALTY
    shrunk = jnp.where(on_diag, stepped, stepped - jnp.clip(stepped, -limit, limit))
    out_ref[...] = shrunk
    if mirrored:
        order_ref, mirror_ref = refs[2:]
        stepped_m = mirror_ref[...] - STEP * (totals[1] / total)
        shrunk_m = stepped_m - jnp.clip(stepped_m, -limit, limit)
        shrunk_m = sum(dot(t, order_ref[...], (1, 1)) for t in split3(shrunk_m)[:2])
        top = shrunk[:, :band]
        out_ref[:, :band] = jnp.where(on_diag[:, :band], top, 0.5 * (top + shrunk_m))
    lane = lax.broadcasted_iota(jnp.int32, sc.shape, 1)
    factor = jnp.where(lane == 0, -1.0, jnp.where(lane == 1, PENALTY, jnp.where(lane == 2, 1.0 / (2.0 * total), 0.0)))
    obj_ref[...] = jnp.sum(sc * factor, axis=1, keepdims=True)


def kernel(fn, outs, in_specs=None):
    specs = {} if in_specs is None else {"in_specs": in_specs}
    return pl.pallas_call(
        fn, out_shape=outs, compiler_params=pltpu.CompilerParams(vmem_limit_bytes=48 * 2**20), **specs
    )


def spread(block, axes, n):
    shape = jax.ShapeDtypeStruct((n,) + block.shape[-2:], jnp.bfloat16)
    return lax.all_to_all(kernel(spread_kernel, shape)(block), axes, 0, 0)


def per_device(counts, coef):
    cells, genes = counts.shape
    cols = coef.shape[1]
    n_dp = N_FAR * N_NEAR
    band = cols * n_dp
    total = float(cells * n_dp)
    tile = lax.axis_index(TILE)
    near = lax.axis_index(NEAR)
    far = lax.axis_index(FAR)
    part = far * N_NEAR + near
    f32, bf16 = jnp.float32, jnp.bfloat16

    coef_t = coef.T
    w_far = spread(coef_t, FAR, N_FAR).reshape(N_FAR * cols, genes)

    place = jnp.stack([tile, part]).astype(jnp.int32)
    lib_rows = cells // LANES
    head, low = pl.pallas_call(
        head_kernel,
        grid=(2,),
        in_specs=[
            pl.BlockSpec(memory_space=pltpu.SMEM),
            pl.BlockSpec((cells // 2, genes), lambda i: (i, 0)),
            pl.BlockSpec((cols, genes), lambda i: (0, 0)),
        ],
        out_specs=[
            pl.BlockSpec((lib_rows // 8 * 8 + 8, LANES), lambda i: (0, 0)),
            pl.BlockSpec((cells // 2, genes), lambda i: (i, 0)),
        ],
        out_shape=[
            jax.ShapeDtypeStruct((lib_rows // 8 * 8 + 8, LANES), f32),
            jax.ShapeDtypeStruct((cells, genes), bf16),
        ],
        compiler_params=pltpu.CompilerParams(vmem_limit_bytes=60 * 2**20),
    )(place, counts, coef_t)

    head = lax.psum(head, "core")
    head = lax.psum(head, "xl")
    w_far, head = lax.optimization_barrier((w_far, head))
    weights = spread(w_far, NEAR, N_NEAR).reshape(band, genes)
    head = lax.psum(head, "y")
    library = head[:lib_rows].reshape(cells)

    scale = SCALE / (library + 1.0)
    expr = jnp.log(1.0 + low.astype(f32) * scale[:, None]).astype(bf16)
    expr = lax.optimization_barrier(expr)
    sums_e = jnp.sum(expr.astype(f32), axis=0, keepdims=True)

    partial = kernel(project_kernel, jax.ShapeDtypeStruct((band, cells), bf16))(weights, expr)
    got = lax.all_to_all(partial.reshape(N_TILE, band // N_TILE, cells), TILE, 0, 0)
    proj = spread(got, TILE, N_TILE).reshape(band, cells)

    head = head[lib_rows : lib_rows + 1]
    rows = N_FAR * cols

    def onehot(at, n):
        return (lax.broadcasted_iota(jnp.int32, (at.shape[0], n), 1) == at[:, None]).astype(bf16)

    coef_m = dot(onehot(part * cols + jnp.arange(cols, dtype=jnp.int32), genes), weights, (1, 1))

    def tail(mirrored):
        wide = genes + (band if mirrored else 0)
        n_picks = 2 if mirrored else 1
        shape = jax.ShapeDtypeStruct((N_NEAR, rows, wide + LANES), bf16)
        got = kernel(functools.partial(pack_kernel, mirrored), shape)(proj, expr, sums_e, head)
        got = lax.all_to_all(got, NEAR, 0, 0)

        slot = jnp.arange(rows, dtype=jnp.int32)
        picks = [near * rows + slot, (slot // cols * N_NEAR + near) * cols + slot % cols]
        picks = [onehot(p, band) for p in picks[:n_picks]]
        shape = jax.ShapeDtypeStruct((N_FAR, cols, wide + 2 * LANES), bf16)
        got = kernel(functools.partial(near_kernel, float(cells), genes), shape)(got, *picks)
        got = lax.all_to_all(got, FAR, 0, 0)

        slot = jnp.arange(cols, dtype=jnp.int32)
        more = [onehot(p + slot, band) for p in (near * rows + far * cols, part * cols)[:n_picks]]
        if mirrored:
            nat = jnp.arange(band, dtype=jnp.int32)
            group = nat // cols
            more.append(onehot((group % N_NEAR * N_FAR + group // N_NEAR) * cols + nat % cols, band))
            more.append(coef_m)
        shapes = (jax.ShapeDtypeStruct((cols, genes), f32), jax.ShapeDtypeStruct((1, 1), f32))
        specs = [pl.BlockSpec(memory_space=pltpu.SMEM)] + [pl.BlockSpec(memory_space=pltpu.VMEM)] * (2 + len(more))
        return kernel(functools.partial(far_kernel, float(cells * N_NEAR), total), shapes, specs)(
            place, got, coef_t, *more
        )

    new_t, objective = lax.cond(tile == 0, lambda: tail(True), lambda: tail(False))
    return (new_t.T, objective[0, 0])


def solution(mesh):
    mesh = Mesh(mesh.devices.reshape(SIZES), AXES)
    return jax.shard_map(
        per_device,
        mesh=mesh,
        in_specs=(P((FAR,) + NEAR, TILE), P(TILE, (FAR,) + NEAR)),
        out_specs=(P(TILE, (FAR,) + NEAR), P()),
        check_vma=False,
    )
```
